32 devices in a mesh: tm: 8 (over z, core), height: 4 (over y, x).
Axes of the slice: x: 2, y: 2, z: 4, core: 2. Of those that a mesh axis runs over, the one named last changes fastest.
Arguments:
- block_input: bfloat16 [16, 8, 160, 384], P('tm', 'height'), may hold values from -400 to 400
- gain: float32 [384], replicated, may hold values from 0.1 to 1.9
- kernel: bfloat16 [384, 10368], P('height'), may hold values from -0.0625 to 0.0625
- cotangent: bfloat16 [16, 8, 160, 384], P('tm', 'height'), may hold values from -11 to 11
Outputs:
- input_grad: bfloat16 [16, 8, 160, 384], P('tm', 'height')
- kernel_grad: float32 [384, 27, 384], P('height', None, 'tm')
- gain_grad: float32 [384], replicated
- bias_grad: float32 [384], replicated
The draws below stay inside these ranges and needn't reach their ends.
All inputs are finite; a program needn't handle non-finite values.
Results may differ from the reference program's by a relative error of at most 0.0029.
Values may be sent and summed in bfloat16 or wider, within the bound.
A program may use at most 128 MiB of HBM per device.

```python
import math
import jax
import jax.numpy as jnp
from jax import lax

C = 384
WIDTH = 160
FRAMES = 16
ROWS = 8


def draw_block_input(key, part):
    key_base, key_cell, key_chan = jax.random.split(jax.random.fold_in(key, 11), 3)
    shape = (FRAMES, ROWS, WIDTH, C)
    cell_scale = jnp.exp(jax.random.uniform(key_cell, (FRAMES, ROWS, WIDTH, 1), jnp.float32) * math.log(10.0))
    base = jnp.clip(jax.random.normal(key_base, shape, jnp.float32), -4.0, 4.0)
    chan_scale = jnp.exp(jax.random.uniform(key_chan, (C,), jnp.float32) * math.log(10.0))
    return (base * cell_scale * chan_scale).astype(jnp.bfloat16)


def draw_cotangent(key, part):
    key_base = jax.random.fold_in(key, 23)
    shape = (FRAMES, ROWS, WIDTH, C)
    frame_pos = jnp.arange(FRAMES, dtype=jnp.float32) / (FRAMES - 1)
    row_pos = jnp.arange(ROWS, dtype=jnp.float32) / (ROWS - 1)
    rising = jnp.exp(math.log(3.0) * (frame_pos[:, None] + row_pos[None, :]))[:, :, None, None]
    base = jnp.clip(jax.random.normal(key_base, shape, jnp.float32), -4.0, 4.0)
    return (0.3 * base * rising).astype(jnp.bfloat16)


def shard_levels(own_key, dims, cuts, least, largest):
    level, own = 1.0, jax.random.fold_in(own_key, 6)
    for position, blocks in cuts:
        steps = jnp.exp(jax.random.uniform(jax.random.fold_in(own, position), (blocks,), jnp.float32, least / len(cuts), largest / len(cuts)))
        level = level * jnp.repeat(steps, dims[position] // blocks).reshape([-1 if axis == position else 1 for axis in range(len(dims))])
    return level


def bell_draw(rng, extent, spread, reach, cuts=(), held_as=jnp.bfloat16):
    values = jax.random.normal(rng, extent, jnp.float32) * spread
    if len(cuts) > 0:
        values = shard_levels(rng, extent, cuts, -0.22, 0.18) * values
    return jnp.clip(values, min=-reach, max=reach).astype(held_as)


def setup_inputs(seed: int = 0) -> dict:
    key_list = jax.random.split(jax.random.key(seed), 5)
    block_input = draw_block_input(jax.random.fold_in(key_list[4], 71), 0)
    gain = jnp.clip(1.0 + 0.18 * jax.random.normal(key_list[1], (C,), jnp.float32), 0.1, 1.9)
    kernel = bell_draw(key_list[2], (C, 27 * C), (27 * C) ** -0.5, 0.0625, ((0, 4),))
    cotangent = draw_cotangent(jax.random.fold_in(key_list[4], 71), 0)
    return dict(block_input=block_input, gain=gain, kernel=kernel, cotangent=cotangent)


def reference(block_input, gain, kernel, cotangent):
    frames, rows, width, chans = block_input.shape
    scale = 1.0 / math.sqrt(frames * rows * width)
    xfull = block_input.astype(jnp.float32)
    inv_rms = lax.rsqrt(lax.optimization_barrier(jnp.mean(xfull * xfull, axis=-1, keepdims=True)) + 1e-06)
    normed = xfull * inv_rms
    pre = normed * gain
    sig = jax.nn.sigmoid(pre)
    act = (pre * sig).astype(jnp.bfloat16)
    act_pad = jnp.pad(act, ((2, 0), (1, 1), (1, 1), (0, 0)))
    grad_pad = jnp.pad(cotangent, ((0, 2), (1, 1), (1, 1), (0, 0)))
    kernel_taps = kernel.reshape(chans, 27, chans)
    grad_flat = cotangent.reshape(-1, chans)
    act_grad = jnp.zeros((frames * rows * width, chans), jnp.float32)
    pieces = []
    for k in range(27):
        ktime, krow, kcol = (k // 9, k // 3 % 3, k % 3)
        act_k = act_pad[ktime:ktime + frames, krow:krow + rows, kcol:kcol + width].reshape(-1, chans)
        pieces.append(lax.dot_general(act_k, grad_flat, (((0,), (0,)), ((), ())), preferred_element_type=jnp.float32))
        grad_k = grad_pad[2 - ktime:2 - ktime + frames, 2 - krow:2 - krow + rows, 2 - kcol:2 - kcol + width].reshape(-1, chans)
        act_grad = act_grad + lax.dot_general(grad_k, kernel_taps[:, k, :], (((1,), (1,)), ((), ())), preferred_element_type=jnp.float32)
    kernel_grad = jnp.stack(pieces, axis=1) * scale
    bias_grad = lax.optimization_barrier(jnp.sum(cotangent.astype(jnp.float32), axis=(0, 1, 2))) * scale
    act_grad = act_grad.reshape(frames, rows, width, chans)
    pre_grad = act_grad * sig * (1.0 + pre * (1.0 - sig))
    gain_grad = lax.optimization_barrier(jnp.sum(pre_grad * normed, axis=(0, 1, 2))) * scale
    normed_grad = pre_grad * gain
    input_grad = inv_rms * (normed_grad - normed * lax.optimization_barrier(jnp.mean(normed_grad * normed, axis=-1, keepdims=True)))
    return (input_grad.astype(jnp.bfloat16), kernel_grad, gain_grad, bias_grad)
```

```python
import functools
import math

import jax
import jax.numpy as jnp
from jax import lax
from jax.experimental import pallas as pl
from jax.experimental.pallas import tpu as pltpu
from jax.sharding import PartitionSpec as P

VMEM_BYTES = 56 * 1024 * 1024


def weight_grad_kernel(width, act_ref, cot_ref, out_ref):
    step = pl.program_id(0)
    ktime, krow = step // 3, step % 3
    own, _, cells = act_ref.shape
    start = pl.multiple_of((2 - krow) * width, 16)
    total = None
    for t in range(own):
        term = jnp.dot(
            act_ref[t],
            cot_ref[t + 2 - ktime, pl.ds(start, cells), :],
            preferred_element_type=jnp.float32,
        )
        total = term if total is None else total + term
    out_ref[0] = total


def weight_grad(act_taps, cot_ext, width):
    own, taps_in, cells = act_taps.shape
    chans = cot_ext.shape[-1]
    return pl.pallas_call(
        functools.partial(weight_grad_kernel, width),
        grid=(9,),
        out_shape=jax.ShapeDtypeStruct((9, taps_in, chans), jnp.float32),
        in_specs=[
            pl.BlockSpec(act_taps.shape, lambda j: (0, 0, 0)),
            pl.BlockSpec(cot_ext.shape, lambda j: (0, 0, 0)),
        ],
        out_specs=pl.BlockSpec((1, taps_in, chans), lambda j: (j, 0, 0)),
        compiler_params=pltpu.CompilerParams(vmem_limit_bytes=VMEM_BYTES),
        cost_estimate=pl.CostEstimate(
            flops=2 * 9 * own * taps_in * cells * chans, bytes_accessed=10**7, transcendentals=0
        ),
    )(act_taps, cot_ext)


def input_conv_kernel(width, cot_ref, kernel_ref, out_ref, total):
    frame, step = pl.program_id(0), pl.program_id(1)
    ktime, krow = step // 3, step % 3
    cells, wide = total.shape
    chans = cot_ref.shape[-1]
    part = wide // 3
    start = pl.multiple_of((2 - krow) * width, 16)
    rows = kernel_ref[...]
    weights = jnp.concatenate([rows[:, c * chans : (c + 1) * chans] for c in range(3)], axis=0)
    term = lax.dot_general(
        cot_ref[frame + 2 - ktime, pl.ds(start, cells), :],
        weights,
        (((1,), (1,)), ((), ())),
        preferred_element_type=jnp.float32,
    )

    @pl.when(step == 0)
    def _():
        total[...] = term

    @pl.when(step > 0)
    def _():
        total[...] += term

    @pl.when(step == 8)
    def _():
        column = lax.rem(lax.broadcasted_iota(jnp.int32, (cells, part), 0), width)
        sums = total[...]
        left = sums[:, :part]
        right = sums[:, 2 * part :]
        left = jnp.where(column == width - 1, 0.0, pltpu.roll(left, cells - 1, 0))
        right = jnp.where(column == 0, 0.0, pltpu.roll(right, 1, 0))
        out_ref[0] = left + sums[:, part : 2 * part] + right


def input_conv(cot_ext, kernel, own, width):
    cells = cot_ext.shape[1] - 2 * width
    chans = cot_ext.shape[2]
    part = kernel.shape[0]
    return pl.pallas_call(
        functools.partial(input_conv_kernel, width),
        grid=(own, 9),
        out_shape=jax.ShapeDtypeStruct((own, cells, part), jnp.float32),
        in_specs=[
            pl.BlockSpec(cot_ext.shape, lambda t, j: (0, 0, 0)),
            pl.BlockSpec((part, 3 * chans), lambda t, j: (0, j)),
        ],
        out_specs=pl.BlockSpec((1, cells, part), lambda t, j: (t, 0, 0)),
        scratch_shapes=[pltpu.VMEM((cells, 3 * part), jnp.float32)],
        compiler_params=pltpu.CompilerParams(vmem_limit_bytes=VMEM_BYTES),
        cost_estimate=pl.CostEstimate(
            flops=2 * own * 27 * cells * chans * part, bytes_accessed=10**7, transcendentals=0
        ),
    )(cot_ext, kernel)


def shards(block_input, gain, kernel, cotangent):
    frames, rows, width, chans = block_input.shape
    high = lax.axis_size("height")
    count = lax.axis_size("tm")
    part = chans // high
    total_rows = rows * high
    scale = 1.0 / math.sqrt(frames * count * total_rows * width)
    xfull = block_input.astype(jnp.float32)
    inv_rms = lax.rsqrt(jnp.mean(xfull * xfull, axis=-1, keepdims=True) + 1e-06)
    normed = xfull * inv_rms
    pre = normed * gain
    sig = jax.nn.sigmoid(pre)
    act = (pre * sig).astype(jnp.bfloat16)

    act_parts = act.reshape(frames, rows, width, high, part).transpose(3, 0, 1, 2, 4)
    act_all = lax.all_to_all(act_parts, "height", 0, 0, tiled=True)
    act_all = act_all.reshape(high, frames, rows, width, part).transpose(1, 0, 2, 3, 4)
    act_all = act_all.reshape(frames, total_rows, width, part)
    cot_all = lax.all_gather(cotangent, "height", axis=1, tiled=True)
    later = lax.ppermute(cot_all, "tm", [(i, i - 1) for i in range(1, count)])
    cot_ext = jnp.concatenate([cot_all, later], axis=0)
    cot_ext = jnp.pad(cot_ext, ((0, 0), (1, 1), (0, 0), (0, 0)))
    cot_ext = cot_ext.reshape(2 * frames, (total_rows + 2) * width, chans)

    act_pad = jnp.pad(act_all, ((0, 0), (0, 0), (1, 1), (0, 0)))
    act_taps = jnp.concatenate([act_pad[:, :, c : c + width] for c in range(3)], axis=-1)
    act_taps = act_taps.reshape(frames, total_rows * width, 3 * part).transpose(0, 2, 1)

    partial = weight_grad(act_taps, cot_ext, width)
    summed = lax.psum_scatter(partial, "tm", scatter_dimension=2, tiled=True)
    kernel_grad = summed.reshape(27, part, chans // count).transpose(1, 0, 2) * scale

    grads = input_conv(cot_ext, kernel, frames, width)
    grads = grads.reshape(frames, high, rows, width, part).transpose(1, 0, 2, 3, 4)
    grads = lax.all_to_all(grads, "height", 0, 0, tiled=True)
    act_grad = grads.transpose(1, 2, 3, 0, 4).reshape(frames, rows, width, chans)

    pre_grad = act_grad * sig * (1.0 + pre * (1.0 - sig))
    gain_local = jnp.sum(pre_grad * normed, axis=(0, 1, 2))
    bias_local = jnp.sum(cotangent.astype(jnp.float32), axis=(0, 1, 2))
    gain_total, bias_total = lax.psum((gain_local, bias_local), ("tm", "height"))
    normed_grad = pre_grad * gain
    input_grad = inv_rms * (
        normed_grad - normed * jnp.mean(normed_grad * normed, axis=-1, keepdims=True)
    )
    return (input_grad.astype(jnp.bfloat16), kernel_grad, gain_total * scale, bias_total * scale)


def solution(mesh):
    return jax.shard_map(
        shards,
        mesh=mesh,
        in_specs=(
            P("tm", "height", None, None),
            P(),
            P("height", None),
            P("tm", "height", None, None),
        ),
        out_specs=(P("tm", "height", None, None), P("height", None, "tm"), P(), P()),
        check_vma=False,
    )
```

```python
import functools
import math

import jax
import jax.numpy as jnp
from jax import lax
from jax.experimental import pallas as pl
from jax.experimental.pallas import tpu as pltpu
from jax.sharding import PartitionSpec as P

VMEM_BYTES = 56 * 1024 * 1024
MESH = pl.DeviceIdType.MESH


def remote(source, target, send, receive, where):
    return pltpu.make_async_remote_copy(
        src_ref=source,
        dst_ref=target,
        send_sem=send,
        recv_sem=receive,
        device_id=where,
        device_id_type=MESH,
    )


def at_place(tm, height):
    return (tm, height)


def exchange_kernel(
    count, high, width, act_ref, cot_ref, act_all, cot_ext, zeros, local_sem, zero_sem,
    act_send, act_recv, cot_send, cot_recv, halo_send, halo_recv,
):
    me, row = lax.axis_index("tm"), lax.axis_index("height")
    frames, block, chans = cot_ref.shape
    whole = high * block
    has_prev, has_next = me > 0, me < count - 1
    barrier = pltpu.get_barrier_semaphore()
    for d in range(1, high):
        pl.semaphore_signal(
            barrier, inc=1, device_id=at_place(me, lax.rem(row + d, high)), device_id_type=MESH
        )

    for step in (1, count - 1):
        pl.semaphore_signal(
            barrier, inc=1, device_id=at_place(lax.rem(me + step, count), row), device_id_type=MESH
        )
    zeros[...] = jnp.zeros_like(zeros)
    pl.semaphore_wait(barrier, high + 1)

    def cot_slot(owner):
        return pl.ds(pl.multiple_of(width + owner * block, 16), block)

    def act_slot(owner):
        return pl.ds(pl.multiple_of(owner * block, 16), block)

    def cot_copy(f, d):
        return remote(
            cot_ref.at[f], cot_ext.at[f, cot_slot(row)],
            cot_send.at[f, d], cot_recv.at[f, d], at_place(me, lax.rem(row + d, high)),
        )

    def halo_copy(f, d):
        slot = cot_slot(lax.rem(row + high - d, high))
        source = cot_ref.at[f] if d == 0 else cot_ext.at[f, slot]
        return remote(
            source, cot_ext.at[frames + f, slot],
            halo_send.at[f, d], halo_recv.at[f, d], at_place(me - 1, row),
        )

    def act_copy(d):
        peer = lax.rem(row + d, high)
        return remote(
            act_ref.at[peer], act_all.at[:, act_slot(row)],
            act_send.at[d], act_recv.at[d], at_place(me, peer),
        )

    locals_ = [
        pltpu.make_async_copy(act_ref.at[row], act_all.at[:, act_slot(row)], local_sem.at[frames])
    ]
    for f in range(frames):
        locals_.append(
            pltpu.make_async_copy(cot_ref.at[f], cot_ext.at[f, cot_slot(row)], local_sem.at[f])
        )
    edges = []
    for f in range(2 * frames):
        for side, start in enumerate((0, width + whole)):
            edges.append(
                pltpu.make_async_copy(
                    zeros.at[pl.ds(0, width)], cot_ext.at[f, pl.ds(start, width)],
                    zero_sem.at[2 * f + side],
                )
            )
    fills = []
    for f in range(frames):
        for r in range(high):
            fills.append(
                pltpu.make_async_copy(
                    zeros, cot_ext.at[frames + f, pl.ds(width + r * block, block)],
                    halo_recv.at[f, r],
                )
            )

    for f in range(frames):
        for d in range(1, high):
            cot_copy(f, d).start()

        @pl.when(has_prev)
        def _():
            halo_copy(f, 0).start()

    for d in range(1, high):
        act_copy(d).start()
    for copy in locals_ + edges:
        copy.start()

    @pl.when(me == count - 1)
    def _():
        for copy in fills:
            copy.start()

    for f in range(frames):
        for d in range(1, high):
            cot_copy(f, d).wait_recv()

            @pl.when(has_prev)
            def _():
                halo_copy(f, d).start()

    for copy in locals_ + edges:
        copy.wait()
    for d in range(1, high):
        act_copy(d).wait()
        for f in range(frames):
            cot_copy(f, d).wait_send()

    @pl.when(has_prev)
    def _():
        for f in range(frames):
            for d in range(high):
                halo_copy(f, d).wait_send()

    @pl.when(has_next)
    def _():
        for f in range(frames):
            for d in range(high):
                halo_copy(f, d).wait_recv()

    @pl.when(me == count - 1)
    def _():
        for copy in fills:
            copy.wait()


def exchange(act_parts, cot, width):
    count, high = lax.axis_size("tm"), lax.axis_size("height")
    frames, block, chans = cot.shape
    part = act_parts.shape[-1]
    anywhere = pl.BlockSpec(memory_space=pl.ANY)
    dma = pltpu.SemaphoreType.DMA
    return pl.pallas_call(
        functools.partial(exchange_kernel, count, high, width),
        out_shape=(
            jax.ShapeDtypeStruct((frames, high * block, part), act_parts.dtype),
            jax.ShapeDtypeStruct((2 * frames, high * block + 2 * width, chans), cot.dtype),
        ),
        in_specs=[anywhere, anywhere],
        out_specs=(anywhere, anywhere),
        scratch_shapes=[
            pltpu.VMEM((block, chans), cot.dtype),
            dma((frames + 1,)),
            dma((4 * frames,)),
            dma((high,)),
            dma((high,)),
            dma((frames, high)),
            dma((frames, high)),
            dma((frames, high)),
            dma((frames, high)),
        ],
        compiler_params=pltpu.CompilerParams(collective_id=0, has_side_effects=True),
    )(act_parts, cot)


def combine_kernel(
    chips, high, scale, partial_ref, grads_ref, out_ref, back_ref, pair_land, send_buf, recv_buf,
    pair_send, pair_recv, chip_send, chip_recv, back_send, back_recv, local_sem,
):
    me, row = lax.axis_index("tm"), lax.axis_index("height")
    chip, core = me // 2, lax.rem(me, 2)
    block = back_ref.shape[2]
    other = chip * 2 + 1 - core
    barrier = pltpu.get_barrier_semaphore()
    pl.semaphore_signal(barrier, inc=1, device_id=at_place(other, row), device_id_type=MESH)
    for k in range(1, chips):
        pl.semaphore_signal(
            barrier, inc=1, device_id=at_place(lax.rem(chip + k, chips) * 2 + core, row),
            device_id_type=MESH,
        )
    for d in range(1, high):
        pl.semaphore_signal(
            barrier, inc=1, device_id=at_place(me, lax.rem(row + d, high)), device_id_type=MESH
        )
    pl.semaphore_wait(barrier, chips + high - 1)

    def pair_copy(k):
        goal = lax.rem(chip + k, chips)
        return remote(
            partial_ref.at[goal * 2 + 1 - core], pair_land.at[k],
            pair_send.at[k], pair_recv.at[k], at_place(other, row),
        )

    def chip_copy(k):
        return remote(
            send_buf.at[k - 1], recv_buf.at[k - 1], chip_send.at[k - 1], chip_recv.at[k - 1],
            at_place(lax.rem(chip + k, chips) * 2 + core, row),
        )

    def part_of(owner):
        return grads_ref.at[:, pl.ds(pl.multiple_of(owner * block, 16), block)]

    def back_copy(d):
        peer = lax.rem(row + d, high)
        return remote(
            part_of(peer), back_ref.at[row], back_send.at[d], back_recv.at[d], at_place(me, peer)
        )

    order = list(range(1, chips)) + [0]
    for k in order:
        pair_copy(k).start()
    for d in range(1, high):
        back_copy(d).start()
    own = pltpu.make_async_copy(part_of(row), back_ref.at[row], local_sem)
    own.start()
    for k in range(1, chips):
        pair_copy(k).wait_recv()
        mine = lax.rem(chip + k, chips) * 2 + core
        send_buf[k - 1] = (partial_ref[mine] + pair_land[k]).astype(send_buf.dtype)
        chip_copy(k).start()
    pair_copy(0).wait_recv()
    out_ref[...] = partial_ref[me] + pair_land[0]
    for k in range(1, chips):
        chip_copy(k).wait_recv()
        out_ref[...] += recv_buf[k - 1].astype(jnp.float32)
    out_ref[...] *= scale
    for k in order:
        pair_copy(k).wait_send()
    for k in range(1, chips):
        chip_copy(k).wait_send()
    for d in range(1, high):
        back_copy(d).wait()
    own.wait()


def combine(partial, grads, rows_block, scale):
    count, high = lax.axis_size("tm"), lax.axis_size("height")
    chips = count // 2
    frames, _, part = grads.shape
    one = partial.shape[1:]
    dma = pltpu.SemaphoreType.DMA
    anywhere = pl.BlockSpec(memory_space=pl.ANY)
    vmem = pl.BlockSpec(memory_space=pltpu.VMEM)
    return pl.pallas_call(
        functools.partial(combine_kernel, chips, high, scale),
        out_shape=(
            jax.ShapeDtypeStruct(one, jnp.float32),
            jax.ShapeDtypeStruct((high, frames, rows_block, part), jnp.float32),
        ),
        in_specs=[vmem, anywhere],
        out_specs=(vmem, anywhere),
        scratch_shapes=[
            pltpu.VMEM((chips,) + one, jnp.float32),
            pltpu.VMEM((chips - 1,) + one, jnp.bfloat16),
            pltpu.VMEM((chips - 1,) + one, jnp.bfloat16),
            dma((chips,)),
            dma((chips,)),
            dma((chips - 1,)),
            dma((chips - 1,)),
            dma((high,)),
            dma((high,)),
            dma,
        ],
        compiler_params=pltpu.CompilerParams(
            collective_id=1, has_side_effects=True, vmem_limit_bytes=VMEM_BYTES
        ),
    )(partial, grads)


def stats_kernel(count, high, local_ref, out_ref, land, middle, across, ts, tr, hs, hr):
    me, row = lax.axis_index("tm"), lax.axis_index("height")
    barrier = pltpu.get_barrier_semaphore()
    for d in range(1, count):
        pl.semaphore_signal(
            barrier, inc=1, device_id=at_place(lax.rem(me + d, count), row), device_id_type=MESH
        )
    for d in range(1, high):
        pl.semaphore_signal(
            barrier, inc=1, device_id=at_place(me, lax.rem(row + d, high)), device_id_type=MESH
        )
    pl.semaphore_wait(barrier, count + high - 2)

    def first(d):
        place = at_place(lax.rem(me + d, count), row)
        return remote(local_ref, land.at[me], ts.at[d], tr.at[d], place)

    def second(d):
        place = at_place(me, lax.rem(row + d, high))
        return remote(middle, across.at[row], hs.at[d], hr.at[d], place)

    for d in range(1, count):
        first(d).start()
    land[me] = local_ref[...]
    for d in range(1, count):
        first(d).wait()
    middle[...] = jnp.sum(land[...], axis=0)
    for d in range(1, high):
        second(d).start()
    across[row] = middle[...]
    for d in range(1, high):
        second(d).wait()
    out_ref[...] = jnp.sum(across[...], axis=0)


def stats_sum(local):
    count, high = lax.axis_size("tm"), lax.axis_size("height")
    vmem = pl.BlockSpec(memory_space=pltpu.VMEM)
    dma = pltpu.SemaphoreType.DMA
    return pl.pallas_call(
        functools.partial(stats_kernel, count, high),
        out_shape=jax.ShapeDtypeStruct(local.shape, local.dtype),
        in_specs=[vmem],
        out_specs=vmem,
        scratch_shapes=[
            pltpu.VMEM((count,) + local.shape, local.dtype),
            pltpu.VMEM(local.shape, local.dtype),
            pltpu.VMEM((high,) + local.shape, local.dtype),
            dma((count,)),
            dma((count,)),
            dma((high,)),
            dma((high,)),
        ],
        compiler_params=pltpu.CompilerParams(collective_id=2, has_side_effects=True),
    )(local)


def weight_grad_kernel(width, act_ref, cot_ref, out_ref):
    step = pl.program_id(0)
    ktime, krow = step // 3, step % 3
    own, _, cells = act_ref.shape
    start = pl.multiple_of((2 - krow) * width, 16)
    total = None
    for t in range(own):
        term = jnp.dot(
            act_ref[t],
            cot_ref[t + 2 - ktime, pl.ds(start, cells), :],
            preferred_element_type=jnp.float32,
        )
        total = term if total is None else total + term
    out_ref[:, 0] = total.T.reshape(out_ref.shape[0], out_ref.shape[2], out_ref.shape[3])


def weight_grad(act_taps, cot_ext, width, count):
    own, taps_in, cells = act_taps.shape
    chans = cot_ext.shape[-1]
    return pl.pallas_call(
        functools.partial(weight_grad_kernel, width),
        grid=(9,),
        out_shape=jax.ShapeDtypeStruct((count, 9, chans // count, taps_in), jnp.float32),
        in_specs=[
            pl.BlockSpec(act_taps.shape, lambda j: (0, 0, 0)),
            pl.BlockSpec(cot_ext.shape, lambda j: (0, 0, 0)),
        ],
        out_specs=pl.BlockSpec((count, 1, chans // count, taps_in), lambda j: (0, j, 0, 0)),
        compiler_params=pltpu.CompilerParams(vmem_limit_bytes=VMEM_BYTES),
        cost_estimate=pl.CostEstimate(
            flops=2 * 9 * own * taps_in * cells * chans, bytes_accessed=10**7, transcendentals=0
        ),
    )(act_taps, cot_ext)


def input_conv_kernel(width, cot_ref, kernel_ref, out_ref, total):
    frame, step = pl.program_id(0), pl.program_id(1)
    ktime, krow = step // 3, step % 3
    cells, wide = total.shape
    chans = cot_ref.shape[-1]
    part = wide // 3
    start = pl.multiple_of((2 - krow) * width, 16)
    rows = kernel_ref[...]
    weights = jnp.concatenate([rows[:, c * chans : (c + 1) * chans] for c in range(3)], axis=0)
    term = lax.dot_general(
        cot_ref[frame + 2 - ktime, pl.ds(start, cells), :],
        weights,
        (((1,), (1,)), ((), ())),
        preferred_element_type=jnp.float32,
    )

    @pl.when(step == 0)
    def _():
        total[...] = term

    @pl.when(step > 0)
    def _():
        total[...] += term

    @pl.when(step == 8)
    def _():
        column = lax.rem(lax.broadcasted_iota(jnp.int32, (cells, part), 0), width)
        sums = total[...]
        left = sums[:, :part]
        right = sums[:, 2 * part :]
        left = jnp.where(column == width - 1, 0.0, pltpu.roll(left, cells - 1, 0))
        right = jnp.where(column == 0, 0.0, pltpu.roll(right, 1, 0))
        out_ref[0] = left + sums[:, part : 2 * part] + right


def input_conv(cot_ext, kernel, own, width):
    cells = cot_ext.shape[1] - 2 * width
    chans = cot_ext.shape[2]
    part = kernel.shape[0]
    return pl.pallas_call(
        functools.partial(input_conv_kernel, width),
        grid=(own, 9),
        out_shape=jax.ShapeDtypeStruct((own, cells, part), jnp.float32),
        in_specs=[
            pl.BlockSpec(cot_ext.shape, lambda t, j: (0, 0, 0)),
            pl.BlockSpec((part, 3 * chans), lambda t, j: (0, j)),
        ],
        out_specs=pl.BlockSpec((1, cells, part), lambda t, j: (t, 0, 0)),
        scratch_shapes=[pltpu.VMEM((cells, 3 * part), jnp.float32)],
        compiler_params=pltpu.CompilerParams(vmem_limit_bytes=VMEM_BYTES),
        cost_estimate=pl.CostEstimate(
            flops=2 * own * 27 * cells * chans * part, bytes_accessed=10**7, transcendentals=0
        ),
    )(cot_ext, kernel)


def shards(block_input, gain, kernel, cotangent):
    frames, rows, width, chans = block_input.shape
    high = lax.axis_size("height")
    count = lax.axis_size("tm")
    part = chans // high
    total_rows = rows * high
    scale = 1.0 / math.sqrt(frames * count * total_rows * width)
    xfull = block_input.astype(jnp.float32)
    inv_rms = lax.rsqrt(jnp.mean(xfull * xfull, axis=-1, keepdims=True) + 1e-06)
    normed = xfull * inv_rms
    pre = normed * gain
    sig = jax.nn.sigmoid(pre)
    act = (pre * sig).astype(jnp.bfloat16)

    act_parts = act.reshape(frames, rows, width, high, part).transpose(3, 0, 1, 2, 4)
    act_parts = act_parts.reshape(high, frames, rows * width, part)
    cot_flat = cotangent.reshape(frames, rows * width, chans)
    act_all, cot_ext = exchange(act_parts, cot_flat, width)
    act_all = act_all.reshape(frames, total_rows, width, part)

    act_pad = jnp.pad(act_all, ((0, 0), (0, 0), (1, 1), (0, 0)))
    act_taps = jnp.concatenate([act_pad[:, :, c : c + width] for c in range(3)], axis=-1)
    act_taps = act_taps.reshape(frames, total_rows * width, 3 * part).transpose(0, 2, 1)

    partial = weight_grad(act_taps, cot_ext, width, count)
    grads = input_conv(cot_ext, kernel, frames, width)
    summed, back = combine(partial, grads, rows * width, scale)
    kernel_grad = summed.reshape(9, chans // count, 3, part).transpose(3, 0, 2, 1)
    kernel_grad = kernel_grad.reshape(part, 27, chans // count)
    act_grad = back.transpose(1, 2, 0, 3).reshape(frames, rows, width, chans)

    pre_grad = act_grad * sig * (1.0 + pre * (1.0 - sig))
    gain_local = jnp.sum(pre_grad * normed, axis=(0, 1, 2))
    bias_local = jnp.sum(cotangent.astype(jnp.float32), axis=(0, 1, 2))
    local = jnp.concatenate(
        [gain_local[None], bias_local[None], jnp.zeros((6, chans), jnp.float32)], axis=0
    )
    totals = stats_sum(local) * scale
    normed_grad = pre_grad * gain
    input_grad = inv_rms * (
        normed_grad - normed * jnp.mean(normed_grad * normed, axis=-1, keepdims=True)
    )
    return (input_grad.astype(jnp.bfloat16), kernel_grad, totals[0], totals[1])


def solution(mesh):
    return jax.shard_map(
        shards,
        mesh=mesh,
        in_specs=(
            P("tm", "height", None, None),
            P(),
            P("height", None),
            P("tm", "height", None, None),
        ),
        out_specs=(P("tm", "height", None, None), P("height", None, "tm"), P(), P()),
        check_vma=False,
    )
```

```python
import functools
import math

import jax
import jax.numpy as jnp
from jax import lax
from jax.experimental import pallas as pl
from jax.experimental.pallas import tpu as pltpu
from jax.sharding import PartitionSpec as P

VMEM_BYTES = 56 * 1024 * 1024
MESH = pl.DeviceIdType.MESH


def remote(source, target, send, receive, where):
    return pltpu.make_async_remote_copy(
        src_ref=source,
        dst_ref=target,
        send_sem=send,
        recv_sem=receive,
        device_id=where,
        device_id_type=MESH,
    )


def at_place(tm, height):
    return (tm, height)


def exchange_kernel(
    count, high, width, act_ref, cot_ref, act_all, cot_ext, zeros, local_sem, zero_sem,
    act_send, act_recv, cot_send, cot_recv, halo_send, halo_recv,
):
    me, row = lax.axis_index("tm"), lax.axis_index("height")
    frames, block, chans = cot_ref.shape
    whole = high * block
    has_prev, has_next = me > 0, me < count - 1
    barrier = pltpu.get_barrier_semaphore()
    for d in range(1, high):
        pl.semaphore_signal(
            barrier, inc=1, device_id=at_place(me, lax.rem(row + d, high)), device_id_type=MESH
        )

    for step in (1, count - 1):
        pl.semaphore_signal(
            barrier, inc=1, device_id=at_place(lax.rem(me + step, count), row), device_id_type=MESH
        )
    zeros[...] = jnp.zeros_like(zeros)
    pl.semaphore_wait(barrier, high + 1)

    def cot_slot(owner):
        return pl.ds(pl.multiple_of(width + owner * block, 16), block)

    def act_slot(owner):
        return pl.ds(pl.multiple_of(owner * block, 16), block)

    def cot_copy(f, d):
        return remote(
            cot_ref.at[f], cot_ext.at[f, cot_slot(row)],
            cot_send.at[f, d], cot_recv.at[f, d], at_place(me, lax.rem(row + d, high)),
        )

    def halo_copy(f, d):
        slot = cot_slot(lax.rem(row + high - d, high))
        source = cot_ref.at[f] if d == 0 else cot_ext.at[f, slot]
        return remote(
            source, cot_ext.at[frames + f, slot],
            halo_send.at[f, d], halo_recv.at[f, d], at_place(me - 1, row),
        )

    def act_copy(d):
        peer = lax.rem(row + d, high)
        return remote(
            act_ref.at[peer], act_all.at[:, act_slot(row)],
            act_send.at[d], act_recv.at[d], at_place(me, peer),
        )

    locals_ = [
        pltpu.make_async_copy(act_ref.at[row], act_all.at[:, act_slot(row)], local_sem.at[frames])
    ]
    for f in range(frames):
        locals_.append(
            pltpu.make_async_copy(cot_ref.at[f], cot_ext.at[f, cot_slot(row)], local_sem.at[f])
        )
    edges = []
    for f in range(2 * frames):
        for side, start in enumerate((0, width + whole)):
            edges.append(
                pltpu.make_async_copy(
                    zeros.at[pl.ds(0, width)], cot_ext.at[f, pl.ds(start, width)],
                    zero_sem.at[2 * f + side],
                )
            )
    fills = []
    for f in range(frames):
        for r in range(high):
            fills.append(
                pltpu.make_async_copy(
                    zeros, cot_ext.at[frames + f, pl.ds(width + r * block, block)],
                    halo_recv.at[f, r],
                )
            )

    for f in range(frames):
        for d in range(1, high):
            cot_copy(f, d).start()

        @pl.when(has_prev)
        def _():
            halo_copy(f, 0).start()

    for d in range(1, high):
        act_copy(d).start()
    for copy in locals_ + edges:
        copy.start()

    @pl.when(me == count - 1)
    def _():
        for copy in fills:
            copy.start()

    for f in range(frames):
        for d in range(1, high):
            cot_copy(f, d).wait_recv()

            @pl.when(has_prev)
            def _():
                halo_copy(f, d).start()

    for copy in locals_ + edges:
        copy.wait()
    for d in range(1, high):
        act_copy(d).wait()
        for f in range(frames):
            cot_copy(f, d).wait_send()

    @pl.when(has_prev)
    def _():
        for f in range(frames):
            for d in range(high):
                halo_copy(f, d).wait_send()

    @pl.when(has_next)
    def _():
        for f in range(frames):
            for d in range(high):
                halo_copy(f, d).wait_recv()

    @pl.when(me == count - 1)
    def _():
        for copy in fills:
            copy.wait()


def exchange(act_parts, cot, width):
    count, high = lax.axis_size("tm"), lax.axis_size("height")
    frames, block, chans = cot.shape
    part = act_parts.shape[-1]
    anywhere = pl.BlockSpec(memory_space=pl.ANY)
    dma = pltpu.SemaphoreType.DMA
    return pl.pallas_call(
        functools.partial(exchange_kernel, count, high, width),
        out_shape=(
            jax.ShapeDtypeStruct((frames, high * block, part), act_parts.dtype),
            jax.ShapeDtypeStruct((2 * frames, high * block + 2 * width, chans), cot.dtype),
        ),
        in_specs=[anywhere, anywhere],
        out_specs=(anywhere, anywhere),
        scratch_shapes=[
            pltpu.VMEM((block, chans), cot.dtype),
            dma((frames + 1,)),
            dma((4 * frames,)),
            dma((high,)),
            dma((high,)),
            dma((frames, high)),
            dma((frames, high)),
            dma((frames, high)),
            dma((frames, high)),
        ],
        compiler_params=pltpu.CompilerParams(collective_id=0, has_side_effects=True),
    )(act_parts, cot)


def finish_kernel(
    count, high, width, scale, partial_ref, cot_ref, kernel_ref, input_ref, gain_ref, bias_ref,
    out_ref, grad_ref, stats_ref,
    weights, grads, back, pair_land, send_buf, recv_buf, local, land, middle, across,
    pair_send, pair_recv, chip_send, chip_recv, back_send, back_recv, ts, tr, hs, hr,
):
    me, row = lax.axis_index("tm"), lax.axis_index("height")
    chip, core = me // 2, lax.rem(me, 2)
    chips = count // 2
    _, frames, block, part = back.shape
    cells = high * block
    chans = cot_ref.shape[-1]
    other = chip * 2 + 1 - core
    barrier = pltpu.get_barrier_semaphore()
    for d in range(1, count):
        pl.semaphore_signal(
            barrier, inc=1, device_id=at_place(lax.rem(me + d, count), row), device_id_type=MESH
        )
    for d in range(1, high):
        pl.semaphore_signal(
            barrier, inc=1, device_id=at_place(me, lax.rem(row + d, high)), device_id_type=MESH
        )
    pl.semaphore_wait(barrier, count + high - 2)

    def pair_copy(k):
        goal = lax.rem(chip + k, chips)
        return remote(
            partial_ref.at[goal * 2 + 1 - core], pair_land.at[k],
            pair_send.at[k], pair_recv.at[k], at_place(other, row),
        )

    def chip_copy(k):
        return remote(
            send_buf.at[k - 1], recv_buf.at[k - 1], chip_send.at[k - 1], chip_recv.at[k - 1],
            at_place(lax.rem(chip + k, chips) * 2 + core, row),
        )

    def part_of(f, owner):
        return grads.at[f, pl.ds(pl.multiple_of(owner * block, 16), block)]

    def back_copy(f, d):
        peer = lax.rem(row + d, high)
        return remote(
            part_of(f, peer), back.at[row, f], back_send.at[f, d], back_recv.at[f, d],
            at_place(me, peer),
        )

    def first(d):
        place = at_place(lax.rem(me + d, count), row)
        return remote(local, land.at[me], ts.at[d], tr.at[d], place)

    def second(d):
        place = at_place(me, lax.rem(row + d, high))
        return remote(middle, across.at[row], hs.at[d], hr.at[d], place)

    order = list(range(1, chips)) + [0]
    for k in order:
        pair_copy(k).start()
    for j in range(9):
        taps = [
            kernel_ref[:, (3 * j + c) * chans : (3 * j + c + 1) * chans] for c in range(3)
        ]
        weights[:, j * chans : (j + 1) * chans] = jnp.concatenate(taps, axis=0)

    span = 2 * block

    def conv(f):
        def body(step, carry):
            left = jnp.concatenate(
                [
                    cot_ref[
                        f + 2 - j // 3,
                        pl.ds(pl.multiple_of(step * span + (2 - j % 3) * width, 16), span),
                        :,
                    ]
                    for j in range(9)
                ],
                axis=1,
            )
            sums = lax.dot_general(
                left, weights[...], (((1,), (1,)), ((), ())), preferred_element_type=jnp.float32
            )
            column = lax.rem(lax.broadcasted_iota(jnp.int32, (span, part), 0), width)
            before = pltpu.roll(sums[:, :part], span - 1, 0)
            after = pltpu.roll(sums[:, 2 * part :], 1, 0)
            grads[f, pl.ds(pl.multiple_of(step * span, 16), span), :] = (
                jnp.where(column == width - 1, 0.0, before)
                + sums[:, part : 2 * part]
                + jnp.where(column == 0, 0.0, after)
            )
            return carry

        lax.fori_loop(0, cells // span, body, 0)
        for d in range(1, high):
            back_copy(f, d).start()
        back[row, f] = part_of(f, row)[...]

    for f in range(frames):
        conv(f)
        if f == 0:
            for k in range(1, chips):
                pair_copy(k).wait_recv()
                mine = lax.rem(chip + k, chips) * 2 + core
                send_buf[k - 1] = (partial_ref[mine] + pair_land[k]).astype(send_buf.dtype)
                chip_copy(k).start()
            pair_copy(0).wait_recv()
            out_ref[...] = partial_ref[me] + pair_land[0]
    for f in range(frames):
        for d in range(1, high):
            back_copy(f, d).wait_recv()

    for f in range(frames):
        wide = high * part
        squares = 0.0
        for h in range(high):
            value = input_ref[h, f].astype(jnp.float32)
            squares = squares + jnp.sum(value * value, axis=-1, keepdims=True)
        inv_rms = lax.rsqrt(squares / wide + 1e-06)
        inner = 0.0
        for h in range(high):
            normed = input_ref[h, f].astype(jnp.float32) * inv_rms
            pre = normed * gain_ref[h]
            sig = jax.nn.sigmoid(pre)
            pre_grad = back[h, f] * sig * (1.0 + pre * (1.0 - sig))
            product = pre_grad * normed
            amount = jnp.sum(product, axis=0, keepdims=True)
            if f == 0:
                local[0, h] = amount
            else:
                local[0, h] += amount
            normed_grad = pre_grad * gain_ref[h]
            inner = inner + jnp.sum(normed_grad * normed, axis=-1, keepdims=True)
            back[h, f] = normed_grad
        if f == frames - 1:
            local[1] = bias_ref[...]
            for d in range(1, count):
                first(d).start()
            land[me] = local[...]
        inner = inner / wide
        for h in range(high):
            normed = input_ref[h, f].astype(jnp.float32) * inv_rms
            grad_ref[h, f] = (inv_rms * (back[h, f] - normed * inner)).astype(grad_ref.dtype)
    for d in range(1, count):
        first(d).wait_recv()
    middle[...] = jnp.sum(land[...], axis=0)
    for d in range(1, high):
        second(d).start()
    across[row] = middle[...]
    for k in range(1, chips):
        chip_copy(k).wait_recv()
        out_ref[...] += recv_buf[k - 1].astype(jnp.float32)
    out_ref[...] *= scale
    for d in range(1, high):
        second(d).wait_recv()
    stats_ref[...] = jnp.sum(across[...], axis=0) * scale
    for k in order:
        pair_copy(k).wait_send()
    for k in range(1, chips):
        chip_copy(k).wait_send()
    for d in range(1, count):
        first(d).wait_send()
    for d in range(1, high):
        second(d).wait_send()
        for f in range(frames):
            back_copy(f, d).wait_send()


def finish(partial, cot_ext, kernel, inputs, gain, bias, width, scale):
    count, high = lax.axis_size("tm"), lax.axis_size("height")
    chips = count // 2
    _, frames, block, part = inputs.shape
    chans = cot_ext.shape[-1]
    one = partial.shape[1:]
    stats = (2,) + bias.shape
    dma = pltpu.SemaphoreType.DMA
    vmem = pl.BlockSpec(memory_space=pltpu.VMEM)
    return pl.pallas_call(
        functools.partial(finish_kernel, count, high, width, scale),
        out_shape=(
            jax.ShapeDtypeStruct(one, jnp.float32),
            jax.ShapeDtypeStruct(inputs.shape, jnp.bfloat16),
            jax.ShapeDtypeStruct(stats, jnp.float32),
        ),
        in_specs=[vmem] * 6,
        out_specs=(vmem,) * 3,
        scratch_shapes=[
            pltpu.VMEM((3 * part, 9 * chans), jnp.bfloat16),
            pltpu.VMEM((frames, high * block, part), jnp.float32),
            pltpu.VMEM((high, frames, block, part), jnp.float32),
            pltpu.VMEM((chips,) + one, jnp.float32),
            pltpu.VMEM((chips - 1,) + one, jnp.bfloat16),
            pltpu.VMEM((chips - 1,) + one, jnp.bfloat16),
            pltpu.VMEM(stats, jnp.float32),
            pltpu.VMEM((count,) + stats, jnp.float32),
            pltpu.VMEM(stats, jnp.float32),
            pltpu.VMEM((high,) + stats, jnp.float32),
            dma((chips,)),
            dma((chips,)),
            dma((chips - 1,)),
            dma((chips - 1,)),
            dma((frames, high)),
            dma((frames, high)),
            dma((count,)),
            dma((count,)),
            dma((high,)),
            dma((high,)),
        ],
        compiler_params=pltpu.CompilerParams(
            collective_id=1, has_side_effects=True, vmem_limit_bytes=VMEM_BYTES
        ),
    )(partial, cot_ext, kernel, inputs, gain, bias)


def weight_grad_kernel(width, act_ref, cot_ref, out_ref):
    step = pl.program_id(0)
    ktime, krow = step // 3, step % 3
    own, _, cells = act_ref.shape
    start = pl.multiple_of((2 - krow) * width, 16)
    total = None
    for t in range(own):
        term = jnp.dot(
            act_ref[t],
            cot_ref[t + 2 - ktime, pl.ds(start, cells), :],
            preferred_element_type=jnp.float32,
        )
        total = term if total is None else total + term
    out_ref[:, 0] = total.T.reshape(out_ref.shape[0], out_ref.shape[2], out_ref.shape[3])


def weight_grad(act_taps, cot_ext, width, count):
    own, taps_in, cells = act_taps.shape
    chans = cot_ext.shape[-1]
    return pl.pallas_call(
        functools.partial(weight_grad_kernel, width),
        grid=(9,),
        out_shape=jax.ShapeDtypeStruct((count, 9, chans // count, taps_in), jnp.float32),
        in_specs=[
            pl.BlockSpec(act_taps.shape, lambda j: (0, 0, 0)),
            pl.BlockSpec(cot_ext.shape, lambda j: (0, 0, 0)),
        ],
        out_specs=pl.BlockSpec((count, 1, chans // count, taps_in), lambda j: (0, j, 0, 0)),
        compiler_params=pltpu.CompilerParams(vmem_limit_bytes=VMEM_BYTES),
        cost_estimate=pl.CostEstimate(
            flops=2 * 9 * own * taps_in * cells * chans, bytes_accessed=10**7, transcendentals=0
        ),
    )(act_taps, cot_ext)


def shards(block_input, gain, kernel, cotangent):
    frames, rows, width, chans = block_input.shape
    high = lax.axis_size("height")
    count = lax.axis_size("tm")
    part = chans // high
    total_rows = rows * high
    scale = 1.0 / math.sqrt(frames * count * total_rows * width)
    xfull = block_input.astype(jnp.float32)
    inv_rms = lax.rsqrt(jnp.mean(xfull * xfull, axis=-1, keepdims=True) + 1e-06)
    normed = xfull * inv_rms
    pre = normed * gain
    sig = jax.nn.sigmoid(pre)
    act = (pre * sig).astype(jnp.bfloat16)

    act_parts = act.reshape(frames, rows, width, high, part).transpose(3, 0, 1, 2, 4)
    act_parts = act_parts.reshape(high, frames, rows * width, part)
    cot_flat = cotangent.reshape(frames, rows * width, chans)
    act_all, cot_ext = exchange(act_parts, cot_flat, width)
    act_all = act_all.reshape(frames, total_rows, width, part)

    act_pad = jnp.pad(act_all, ((0, 0), (0, 0), (1, 1), (0, 0)))
    act_taps = jnp.concatenate([act_pad[:, :, c : c + width] for c in range(3)], axis=-1)
    act_taps = act_taps.reshape(frames, total_rows * width, 3 * part).transpose(0, 2, 1)

    partial = weight_grad(act_taps, cot_ext, width, count)
    bias = jnp.sum(cotangent.astype(jnp.float32), axis=(0, 1, 2)).reshape(high, 1, part)
    inputs = block_input.reshape(frames, rows * width, high, part).transpose(2, 0, 1, 3)
    summed, grads, totals = finish(
        partial, cot_ext, kernel, inputs, gain.reshape(high, 1, part), bias, width, scale
    )
    kernel_grad = summed.reshape(9, chans // count, 3, part).transpose(3, 0, 2, 1)
    kernel_grad = kernel_grad.reshape(part, 27, chans // count)
    input_grad = grads.transpose(1, 2, 0, 3).reshape(frames, rows, width, chans)
    totals = totals.reshape(2, chans)
    return (input_grad, kernel_grad, totals[0], totals[1])


def solution(mesh):
    return jax.shard_map(
        shards,
        mesh=mesh,
        in_specs=(
            P("tm", "height", None, None),
            P(),
            P("height", None),
            P("tm", "height", None, None),
        ),
        out_specs=(P("tm", "height", None, None), P("height", None, "tm"), P(), P()),
        check_vma=False,
    )
```

```python
import functools
import math

import jax
import jax.numpy as jnp
from jax import lax
from jax.experimental import pallas as pl
from jax.experimental.pallas import tpu as pltpu
from jax.sharding import PartitionSpec as P

VMEM_BYTES = 56 * 1024 * 1024
MESH = pl.DeviceIdType.MESH


def remote(source, target, send, receive, where):
    return pltpu.make_async_remote_copy(
        src_ref=source,
        dst_ref=target,
        send_sem=send,
        recv_sem=receive,
        device_id=where,
        device_id_type=MESH,
    )


def at_place(tm, height):
    return (tm, height)


def exchange_kernel(
    count, high, width, act_ref, cot_ref, act_all, cot_ext, zeros, local_sem, zero_sem,
    act_send, act_recv, cot_send, cot_recv, halo_send, halo_recv,
):
    me, row = lax.axis_index("tm"), lax.axis_index("height")
    frames, block, chans = cot_ref.shape
    whole = high * block
    has_prev, has_next = me > 0, me < count - 1
    barrier = pltpu.get_barrier_semaphore()
    for d in range(1, high):
        pl.semaphore_signal(
            barrier, inc=1, device_id=at_place(me, lax.rem(row + d, high)), device_id_type=MESH
        )

    for step in (1, count - 1):
        pl.semaphore_signal(
            barrier, inc=1, device_id=at_place(lax.rem(me + step, count), row), device_id_type=MESH
        )
    zeros[...] = jnp.zeros_like(zeros)
    pl.semaphore_wait(barrier, high + 1)

    def cot_slot(owner):
        return pl.ds(pl.multiple_of(width + owner * block, 16), block)

    def act_slot(owner):
        return pl.ds(pl.multiple_of(owner * block, 16), block)

    def cot_copy(f, d):
        return remote(
            cot_ref.at[f], cot_ext.at[f, cot_slot(row)],
            cot_send.at[f, d], cot_recv.at[f, d], at_place(me, lax.rem(row + d, high)),
        )

    def halo_copy(f, d):
        slot = cot_slot(lax.rem(row + high - d, high))
        source = cot_ref.at[f] if d == 0 else cot_ext.at[f, slot]
        return remote(
            source, cot_ext.at[frames + f, slot],
            halo_send.at[f, d], halo_recv.at[f, d], at_place(me - 1, row),
        )

    def act_copy(d):
        peer = lax.rem(row + d, high)
        return remote(
            act_ref.at[peer], act_all.at[:, act_slot(row)],
            act_send.at[d], act_recv.at[d], at_place(me, peer),
        )

    locals_ = [
        pltpu.make_async_copy(act_ref.at[row], act_all.at[:, act_slot(row)], local_sem.at[frames])
    ]
    for f in range(frames):
        locals_.append(
            pltpu.make_async_copy(cot_ref.at[f], cot_ext.at[f, cot_slot(row)], local_sem.at[f])
        )
    edges = []
    for f in range(2 * frames):
        for side, start in enumerate((0, width + whole)):
            edges.append(
                pltpu.make_async_copy(
                    zeros.at[pl.ds(0, width)], cot_ext.at[f, pl.ds(start, width)],
                    zero_sem.at[2 * f + side],
                )
            )
    fills = []
    for f in range(frames):
        for r in range(high):
            fills.append(
                pltpu.make_async_copy(
                    zeros, cot_ext.at[frames + f, pl.ds(width + r * block, block)],
                    halo_recv.at[f, r],
                )
            )

    for f in range(frames):
        for d in range(1, high):
            cot_copy(f, d).start()

        @pl.when(has_prev)
        def _():
            halo_copy(f, 0).start()

    for d in range(1, high):
        act_copy(d).start()
    for copy in locals_ + edges:
        copy.start()

    @pl.when(me == count - 1)
    def _():
        for copy in fills:
            copy.start()

    for f in range(frames):
        for d in range(1, high):
            cot_copy(f, d).wait_recv()

            @pl.when(has_prev)
            def _():
                halo_copy(f, d).start()

    for copy in locals_ + edges:
        copy.wait()
    for d in range(1, high):
        act_copy(d).wait()
        for f in range(frames):
            cot_copy(f, d).wait_send()

    @pl.when(has_prev)
    def _():
        for f in range(frames):
            for d in range(high):
                halo_copy(f, d).wait_send()

    @pl.when(has_next)
    def _():
        for f in range(frames):
            for d in range(high):
                halo_copy(f, d).wait_recv()

    @pl.when(me == count - 1)
    def _():
        for copy in fills:
            copy.wait()


def exchange(act_parts, cot, width):
    count, high = lax.axis_size("tm"), lax.axis_size("height")
    frames, block, chans = cot.shape
    part = act_parts.shape[-1]
    anywhere = pl.BlockSpec(memory_space=pl.ANY)
    dma = pltpu.SemaphoreType.DMA
    return pl.pallas_call(
        functools.partial(exchange_kernel, count, high, width),
        out_shape=(
            jax.ShapeDtypeStruct((frames, high * block, part), act_parts.dtype),
            jax.ShapeDtypeStruct((2 * frames, high * block + 2 * width, chans), cot.dtype),
        ),
        in_specs=[anywhere, anywhere],
        out_specs=(anywhere, anywhere),
        scratch_shapes=[
            pltpu.VMEM((block, chans), cot.dtype),
            dma((frames + 1,)),
            dma((4 * frames,)),
            dma((high,)),
            dma((high,)),
            dma((frames, high)),
            dma((frames, high)),
            dma((frames, high)),
            dma((frames, high)),
        ],
        compiler_params=pltpu.CompilerParams(collective_id=0, has_side_effects=True),
    )(act_parts, cot)


def finish_kernel(
    count, high, width, scale, partial_ref, cot_ref, kernel_ref, input_ref, gain_ref, bias_ref,
    out_ref, grad_ref, stats_ref,
    weights, grads, back, pair_land, send_buf, recv_buf, local, land, middle, across,
    pair_send, pair_recv, chip_send, chip_recv, back_send, back_recv, ts, tr, hs, hr,
):
    me, row = lax.axis_index("tm"), lax.axis_index("height")
    chip, core = me // 2, lax.rem(me, 2)
    chips = count // 2
    _, frames, block, part = back.shape
    cells = high * block
    chans = cot_ref.shape[-1]
    other = chip * 2 + 1 - core
    barrier = pltpu.get_barrier_semaphore()
    for d in range(1, count):
        pl.semaphore_signal(
            barrier, inc=1, device_id=at_place(lax.rem(me + d, count), row), device_id_type=MESH
        )
    for d in range(1, high):
        pl.semaphore_signal(
            barrier, inc=1, device_id=at_place(me, lax.rem(row + d, high)), device_id_type=MESH
        )
    pl.semaphore_wait(barrier, count + high - 2)

    def pair_copy(k):
        goal = lax.rem(chip + k, chips)
        return remote(
            partial_ref.at[goal * 2 + 1 - core], pair_land.at[k],
            pair_send.at[k], pair_recv.at[k], at_place(other, row),
        )

    def chip_copy(k):
        return remote(
            send_buf.at[k - 1], recv_buf.at[k - 1], chip_send.at[k - 1], chip_recv.at[k - 1],
            at_place(lax.rem(chip + k, chips) * 2 + core, row),
        )

    def part_of(f, owner):
        return grads.at[f, pl.ds(pl.multiple_of(owner * block, 16), block)]

    def back_copy(f, d):
        peer = lax.rem(row + d, high)
        return remote(
            part_of(f, peer), back.at[row, f], back_send.at[f, d], back_recv.at[f, d],
            at_place(me, peer),
        )

    def first(d):
        place = at_place(lax.rem(me + d, count), row)
        return remote(local, land.at[me], ts.at[d], tr.at[d], place)

    def second(d):
        place = at_place(me, lax.rem(row + d, high))
        return remote(middle, across.at[row], hs.at[d], hr.at[d], place)

    order = list(range(1, chips)) + [0]
    for k in order:
        pair_copy(k).start()
    for j in range(9):
        taps = [
            kernel_ref[:, (3 * j + c) * chans : (3 * j + c + 1) * chans] for c in range(3)
        ]
        weights[:, j * chans : (j + 1) * chans] = jnp.concatenate(taps, axis=0)

    span = 2 * block

    def conv(f, low, top):
        def body(step, carry):
            left = jnp.concatenate(
                [
                    cot_ref[
                        f + 2 - j // 3,
                        pl.ds(pl.multiple_of(step * span + (2 - j % 3) * width, 16), span),
                        :,
                    ]
                    for j in range(9)
                ],
                axis=1,
            )
            sums = lax.dot_general(
                left, weights[...], (((1,), (1,)), ((), ())), preferred_element_type=jnp.float32
            )
            column = lax.rem(lax.broadcasted_iota(jnp.int32, (span, part), 0), width)
            before = pltpu.roll(sums[:, :part], span - 1, 0)
            after = pltpu.roll(sums[:, 2 * part :], 1, 0)
            grads[f, pl.ds(pl.multiple_of(step * span, 16), span), :] = (
                jnp.where(column == width - 1, 0.0, before)
                + sums[:, part : 2 * part]
                + jnp.where(column == 0, 0.0, after)
            )
            return carry

        lax.fori_loop(low, top, body, 0)

    def send_back(f):
        for d in range(1, high):
            back_copy(f, d).start()
        back[row, f] = part_of(f, row)[...]

    conv(0, 0, 1)
    for k in range(1, chips):
        pair_copy(k).wait_recv()
        mine = lax.rem(chip + k, chips) * 2 + core
        for g in range(3):
            sums = [partial_ref[mine, 3 * g + j] + pair_land[k, 3 * g + j] for j in range(3)]
            send_buf[k - 1, g] = jnp.concatenate(sums, axis=-1).astype(send_buf.dtype)
        chip_copy(k).start()
    conv(0, 1, cells // span)
    send_back(0)
    for f in range(1, frames):
        conv(f, 0, cells // span)
        send_back(f)
    pair_copy(0).wait_recv()
    out_ref[...] = partial_ref[me] + pair_land[0]
    for f in range(frames):
        for d in range(1, high):
            back_copy(f, d).wait_recv()

    for f in range(frames):
        wide = high * part
        squares = 0.0
        for h in range(high):
            value = input_ref[h, f].astype(jnp.float32)
            squares = squares + jnp.sum(value * value, axis=-1, keepdims=True)
        inv_rms = lax.rsqrt(squares / wide + 1e-06)
        inner = 0.0
        for h in range(high):
            normed = input_ref[h, f].astype(jnp.float32) * inv_rms
            pre = normed * gain_ref[h]
            sig = jax.nn.sigmoid(pre)
            pre_grad = back[h, f] * sig * (1.0 + pre * (1.0 - sig))
            product = pre_grad * normed
            amount = jnp.sum(product, axis=0, keepdims=True)
            if f == 0:
                local[0, h] = amount
            else:
                local[0, h] += amount
            normed_grad = pre_grad * gain_ref[h]
            inner = inner + jnp.sum(normed_grad * normed, axis=-1, keepdims=True)
            back[h, f] = normed_grad
        if f == frames - 1:
            local[1] = bias_ref[...]
            for d in range(1, count):
                first(d).start()
            land[me] = local[...]
        inner = inner / wide
        for h in range(high):
            normed = input_ref[h, f].astype(jnp.float32) * inv_rms
            grad_ref[h, f] = (inv_rms * (back[h, f] - normed * inner)).astype(grad_ref.dtype)
    for d in range(1, count):
        first(d).wait_recv()
    middle[...] = jnp.sum(land[...], axis=0)
    for d in range(1, high):
        second(d).start()
    across[row] = middle[...]
    for k in range(1, chips):
        chip_copy(k).wait_recv()
        for g in range(3):
            terms = recv_buf[k - 1, g].astype(jnp.float32)
            for j in range(3):
                out_ref[3 * g + j] += terms[:, j * 3 * part : (j + 1) * 3 * part]
    out_ref[...] *= scale
    for d in range(1, high):
        second(d).wait_recv()
    stats_ref[...] = jnp.sum(across[...], axis=0) * scale
    for k in order:
        pair_copy(k).wait_send()
    for k in range(1, chips):
        chip_copy(k).wait_send()
    for d in range(1, count):
        first(d).wait_send()
    for d in range(1, high):
        second(d).wait_send()
        for f in range(frames):
            back_copy(f, d).wait_send()


def finish(partial, cot_ext, kernel, inputs, gain, bias, width, scale):
    count, high = lax.axis_size("tm"), lax.axis_size("height")
    chips = count // 2
    _, frames, block, part = inputs.shape
    chans = cot_ext.shape[-1]
    one = partial.shape[1:]
    stats = (2,) + bias.shape
    dma = pltpu.SemaphoreType.DMA
    vmem = pl.BlockSpec(memory_space=pltpu.VMEM)
    return pl.pallas_call(
        functools.partial(finish_kernel, count, high, width, scale),
        out_shape=(
            jax.ShapeDtypeStruct(one, jnp.float32),
            jax.ShapeDtypeStruct(inputs.shape, jnp.bfloat16),
            jax.ShapeDtypeStruct(stats, jnp.float32),
        ),
        in_specs=[vmem] * 6,
        out_specs=(vmem,) * 3,
        scratch_shapes=[
            pltpu.VMEM((3 * part, 9 * chans), jnp.bfloat16),
            pltpu.VMEM((frames, high * block, part), jnp.float32),
            pltpu.VMEM((high, frames, block, part), jnp.float32),
            pltpu.VMEM((chips,) + one, jnp.float32),
            pltpu.VMEM((chips - 1, 3, one[1], 9 * part), jnp.bfloat16),
            pltpu.VMEM((chips - 1, 3, one[1], 9 * part), jnp.bfloat16),
            pltpu.VMEM(stats, jnp.float32),
            pltpu.VMEM((count,) + stats, jnp.float32),
            pltpu.VMEM(stats, jnp.float32),
            pltpu.VMEM((high,) + stats, jnp.float32),
            dma((chips,)),
            dma((chips,)),
            dma((chips - 1,)),
            dma((chips - 1,)),
            dma((frames, high)),
            dma((frames, high)),
            dma((count,)),
            dma((count,)),
            dma((high,)),
            dma((high,)),
        ],
        compiler_params=pltpu.CompilerParams(
            collective_id=1, has_side_effects=True, vmem_limit_bytes=VMEM_BYTES
        ),
    )(partial, cot_ext, kernel, inputs, gain, bias)


def weight_grad_kernel(width, act_ref, cot_ref, out_ref):
    step = pl.program_id(0)
    ktime, krow = step // 3, step % 3
    own, _, cells = act_ref.shape
    start = pl.multiple_of((2 - krow) * width, 16)
    total = None
    for t in range(own):
        term = jnp.dot(
            act_ref[t],
            cot_ref[t + 2 - ktime, pl.ds(start, cells), :],
            preferred_element_type=jnp.float32,
        )
        total = term if total is None else total + term
    out_ref[:, 0] = total.T.reshape(out_ref.shape[0], out_ref.shape[2], out_ref.shape[3])


def weight_grad(act_taps, cot_ext, width, count):
    own, taps_in, cells = act_taps.shape
    chans = cot_ext.shape[-1]
    return pl.pallas_call(
        functools.partial(weight_grad_kernel, width),
        grid=(9,),
        out_shape=jax.ShapeDtypeStruct((count, 9, chans // count, taps_in), jnp.float32),
        in_specs=[
            pl.BlockSpec(act_taps.shape, lambda j: (0, 0, 0)),
            pl.BlockSpec(cot_ext.shape, lambda j: (0, 0, 0)),
        ],
        out_specs=pl.BlockSpec((count, 1, chans // count, taps_in), lambda j: (0, j, 0, 0)),
        compiler_params=pltpu.CompilerParams(vmem_limit_bytes=VMEM_BYTES),
        cost_estimate=pl.CostEstimate(
            flops=2 * 9 * own * taps_in * cells * chans, bytes_accessed=10**7, transcendentals=0
        ),
    )(act_taps, cot_ext)


def shards(block_input, gain, kernel, cotangent):
    frames, rows, width, chans = block_input.shape
    high = lax.axis_size("height")
    count = lax.axis_size("tm")
    part = chans // high
    total_rows = rows * high
    scale = 1.0 / math.sqrt(frames * count * total_rows * width)
    xfull = block_input.astype(jnp.float32)
    inv_rms = lax.rsqrt(jnp.mean(xfull * xfull, axis=-1, keepdims=True) + 1e-06)
    normed = xfull * inv_rms
    pre = normed * gain
    sig = jax.nn.sigmoid(pre)
    act = (pre * sig).astype(jnp.bfloat16)

    act_parts = act.reshape(frames, rows, width, high, part).transpose(3, 0, 1, 2, 4)
    act_parts = act_parts.reshape(high, frames, rows * width, part)
    cot_flat = cotangent.reshape(frames, rows * width, chans)
    act_all, cot_ext = exchange(act_parts, cot_flat, width)
    act_all = act_all.reshape(frames, total_rows, width, part)

    act_pad = jnp.pad(act_all, ((0, 0), (0, 0), (1, 1), (0, 0)))
    act_taps = jnp.concatenate([act_pad[:, :, c : c + width] for c in range(3)], axis=-1)
    act_taps = act_taps.reshape(frames, total_rows * width, 3 * part).transpose(0, 2, 1)

    partial = weight_grad(act_taps, cot_ext, width, count)
    bias = jnp.sum(cotangent.astype(jnp.float32), axis=(0, 1, 2)).reshape(high, 1, part)
    inputs = block_input.reshape(frames, rows * width, high, part).transpose(2, 0, 1, 3)
    summed, grads, totals = finish(
        partial, cot_ext, kernel, inputs, gain.reshape(high, 1, part), bias, width, scale
    )
    kernel_grad = summed.reshape(9, chans // count, 3, part).transpose(3, 0, 2, 1)
    kernel_grad = kernel_grad.reshape(part, 27, chans // count)
    input_grad = grads.transpose(1, 2, 0, 3).reshape(frames, rows, width, chans)
    totals = totals.reshape(2, chans)
    return (input_grad, kernel_grad, totals[0], totals[1])


def solution(mesh):
    return jax.shard_map(
        shards,
        mesh=mesh,
        in_specs=(
            P("tm", "height", None, None),
            P(),
            P("height", None),
            P("tm", "height", None, None),
        ),
        out_specs=(P("tm", "height", None, None), P("height", None, "tm"), P(), P()),
        check_vma=False,
    )
```
